512 devices in a mesh: sub: 64 (over y, z_lo, core), grp: 8 (over x, z_hi).
Axes of the slice: x: 4, y: 8, z: 8 (z_hi: 2, z_lo: 4; z = z_hi * 4 + z_lo), core: 2. Of those that a mesh axis runs over, the one named last changes fastest.
Arguments:
- front_trail: float32 [16384, 16384], P('sub', 'grp'), may hold values from -6 to 6
- front_below: float32 [16384, 1024], P('sub', 'grp'), may hold values from -6 to 6
- front_pivot: float32 [1024, 1024], P('sub', 'grp'), may hold values from -0.02 to 5, as said below
- panel_mask: int32 [64], P('sub'), may hold values 0 or 1
- child_tiles: float32 [64, 8, 2, 256, 256], P('sub', 'grp'), may hold values from -6 to 6
- child_slot: int32 [64, 8, 2], P('sub', 'grp'), may hold values from 0 to 7
- child_far: int32 [64, 8, 2], P('sub', 'grp'), may hold values 0 or 1
Outputs:
- schur_block: float32 [16384, 16384], P('sub', 'grp')
- panel: float32 [16384, 1024], P('sub', 'grp')
The draws below stay inside these ranges and needn't reach their ends.
Inputs may be any that keep to these rules, and one draw needn't show every extreme that they name: `front_pivot`: symmetric positive definite.
All inputs are finite; a program needn't handle non-finite values. No bound on the sum of `panel_mask` or of `child_far` on one device may be relied on, other than what follows from the above.
Results may differ from the reference program's by a relative error of at most 0.0018.
The reference program's roundings to bfloat16 on the way (of `rounded_panel`) count: a program that leaves them out, or rounds other values in their place, can miss the bound.
Values may be sent and summed in bfloat16 or wider, within the bound.
A program may use at most 128 MiB of HBM per device.

```python
import math
import jax
import jax.numpy as jnp
from jax import lax

TILE = 256
PW = 1024
NU = 16384
UT = 2
NT = 64
N_SUB = 64
N_GRP = 8


def draw_front_pivot(key, part):
    key = jax.random.fold_in(key, 11)
    key_noise, key_scale = jax.random.split(key)
    decay_rate = 0.9
    scale_low = 0.7
    scale_high = 1.4
    position = jnp.arange(PW, dtype=jnp.float32)
    distance = jnp.abs(position[:, None] - position[None, :])
    kernel = jnp.exp(distance * math.log(decay_rate))
    noise_bound = 0.1 / PW ** 0.5
    raw_noise = jax.random.uniform(key_noise, (PW, PW), jnp.float32, -noise_bound, noise_bound)
    sym_noise = 0.5 * (raw_noise + raw_noise.T)
    identity = jnp.eye(PW, dtype=jnp.float32)
    core_matrix = kernel + sym_noise + 0.2 * identity
    row_scales = jnp.exp(jax.random.uniform(key_scale, (PW,), jnp.float32, math.log(scale_low), math.log(scale_high)))
    return core_matrix * row_scales[:, None] * row_scales[None, :]


def with_ends(drawn, stream_key, least, top_value):
    longest = drawn.shape.index(max(drawn.shape))
    spots = []
    for shift in (0, 1):
        where = [jax.random.randint(jax.random.fold_in(stream_key, axis), (), 0, length) for axis, length in enumerate(drawn.shape)]
        where[longest] = (where[longest] + shift) % drawn.shape[longest]
        spots.append(tuple(where))
    return drawn.at[spots[0]].set(least).at[spots[1]].set(top_value)


def shard_levels(stream_key, extent, shards, smallest, largest):
    factor_of, own = 1.0, jax.random.fold_in(stream_key, 6)
    for axis_at, parts in shards:
        steps = jnp.exp(jax.random.uniform(jax.random.fold_in(own, axis_at), (parts,), jnp.float32, smallest / len(shards), largest / len(shards)))
        factor_of = factor_of * jnp.repeat(steps, extent[axis_at] // parts).reshape([-1 if axis == axis_at else 1 for axis in range(len(extent))])
    return factor_of


def normal_values(stream_key, shape, deviation, limit, cuts=(), kind=jnp.bfloat16):
    array = deviation * jax.random.normal(stream_key, shape, jnp.float32)
    if cuts:
        array = array * shard_levels(stream_key, shape, cuts, -0.22, 0.18)
    return jnp.clip(array, -limit, limit).astype(kind)


def setup_inputs(seed: int = 0) -> dict:
    key_list = jax.random.split(jax.random.key(seed), 8)
    return {
        "front_trail": normal_values(key_list[0], (NU, NU), 1.0, 6.0, ((0, 64), (1, 8)), jnp.float32),
        "front_below": normal_values(key_list[1], (NU, PW), 1.0, 6.0, ((0, 64), (1, 8)), jnp.float32),
        "front_pivot": draw_front_pivot(jax.random.fold_in(key_list[7], 71), 0),
        "panel_mask": with_ends((jax.random.randint(key_list[3], (NT,), 0, 4) < 3).astype(jnp.int32), jax.random.fold_in(key_list[3], 1), 0, 1),
        "child_tiles": normal_values(key_list[4], (N_SUB, N_GRP, UT, TILE, TILE), 1.0, 6.0, ((0, 64), (1, 8)), jnp.float32),
        "child_slot": with_ends(jax.random.randint(key_list[5], (N_SUB, N_GRP, UT), 0, (NU // (TILE * N_SUB)) * (NU // (TILE * N_GRP))), jax.random.fold_in(key_list[5], 1), 0, ((NU // (TILE * N_SUB)) * (NU // (TILE * N_GRP))) - 1).astype(jnp.int32),
        "child_far": with_ends((jax.random.randint(key_list[6], (N_SUB, N_GRP, UT), 0, 2) < 1).astype(jnp.int32), jax.random.fold_in(key_list[6], 1), 0, 1),
    }


def reference(front_trail, front_below, front_pivot, panel_mask, child_tiles, child_slot, child_far):
    rows_dev = NU // N_SUB
    cols_dev = NU // N_GRP
    tiles_row = rows_dev // TILE
    tiles_col = cols_dev // TILE
    sub_ids = jnp.arange(N_SUB, dtype=jnp.int32)[:, None, None]
    grp_ids = jnp.arange(N_GRP, dtype=jnp.int32)[None, :, None]
    target = jnp.bitwise_xor(sub_ids, child_far * (N_SUB // 2)).astype(jnp.int32)
    grp_full = jnp.broadcast_to(grp_ids, child_slot.shape).astype(jnp.int32)
    tile_grid = jnp.zeros((N_SUB, N_GRP, tiles_row * tiles_col, TILE, TILE), jnp.float32)
    tile_grid = tile_grid.at[target, grp_full, child_slot].add(child_tiles)
    added = tile_grid.reshape(N_SUB, N_GRP, tiles_row, tiles_col, TILE, TILE)
    added = added.transpose(0, 2, 4, 1, 3, 5).reshape(NU, NU)
    assembled = front_trail + added
    pivot_factor = jnp.linalg.cholesky(front_pivot)
    row_keep = jnp.repeat(panel_mask, TILE).astype(jnp.float32)
    masked = front_below * row_keep[:, None]
    panel = jax.scipy.linalg.solve_triangular(pivot_factor, masked.T, lower=True).T
    rounded_panel = panel.astype(jnp.bfloat16)
    wide_panel = rounded_panel.astype(jnp.float32)
    block_rows = math.gcd(NU, 1024)

    def row_block(rows_in):
        return jnp.dot(rows_in.astype(jnp.float32), wide_panel.T.astype(jnp.float32), precision=lax.Precision.HIGHEST, preferred_element_type=jnp.float32)
    update = lax.map(row_block, wide_panel.reshape(NU // block_rows, block_rows, PW)).reshape(NU, NU)
    schur_block = assembled - update
    return (schur_block, panel)
```

```python
import jax
import jax.numpy as jnp
from jax import lax
from jax.experimental import pallas as pl
from jax.experimental.pallas import tpu as pltpu
from jax.sharding import PartitionSpec as P

F32, BF16 = jnp.float32, jnp.bfloat16
MESH = pl.DeviceIdType.MESH
NB = 8


def row_of(v, r):
    return jnp.broadcast_to(v[r : r + 1, :], v.shape)


def lane_of(v, c):
    return jnp.broadcast_to(v[:, c : c + 1], v.shape)


def inverse_factor(block):
    strips = block.shape[0] // 8
    width = block.shape[1]
    sub = lax.broadcasted_iota(jnp.int32, (8, width), 0)
    lane = lax.broadcasted_iota(jnp.int32, (8, width), 1)
    unit = [(lane == sub + 8 * t).astype(F32) for t in range(strips)]
    left = [block[8 * t : 8 * t + 8, :] for t in range(strips)]
    out = []
    for k in range(strips):
        pivot, jordan, forward = left[k], unit[k], unit[k]
        cols = [lane_of(pivot, 8 * k + c) for c in range(8)]
        diag = jnp.ones((8, width), F32)
        for r in range(0, 8, 2):
            a = row_of(cols[r], r)
            b = row_of(cols[r], r + 1)
            d = row_of(cols[r + 1], r + 1)
            det = a * d - b * b
            over = 1.0 / det
            over_a = 1.0 / a
            ia, ib, id_ = d * over, -b * over, a * over
            is0, is1 = sub == r, sub == r + 1
            pair = is0 | is1
            g0 = jnp.where(is0, -ia, jnp.where(is1, -ib, cols[r] * ia + cols[r + 1] * ib))
            g1 = jnp.where(is0, -ib, jnp.where(is1, -id_, cols[r] * ib + cols[r + 1] * id_))
            f0, f1 = row_of(forward, r), row_of(forward, r + 1)
            forward = jnp.where(
                sub > r + 1,
                forward - g0 * f0 - g1 * f1,
                jnp.where(is1, forward - (b * over_a) * f0, forward),
            )
            diag = jnp.where(is0, a, jnp.where(is1, det * over_a, diag))

            def step(v):
                return (jnp.where(pair, 0.0, v) - g0 * row_of(v, r)) - g1 * row_of(v, r + 1)

            for c in range(r + 2, 8):
                cols[c] = step(cols[c])
            jordan, pivot = step(jordan), step(pivot)
        out.append(forward * lax.rsqrt(diag))
        prow = [row_of(pivot, c) for c in range(8)]
        jrow = [row_of(jordan, c) for c in range(8)]
        for t in range(k + 1, strips):
            coef = [lane_of(left[t], 8 * k + c) for c in range(8)]

            def total(q):
                p = [coef[c] * q[c] for c in range(8)]
                return ((p[0] + p[1]) + (p[2] + p[3])) + ((p[4] + p[5]) + (p[6] + p[7]))

            left[t] = left[t] - total(prow)
            unit[t] = unit[t] - total(jrow)
    return jnp.concatenate(out, axis=0)


def split(v):
    hi = v.astype(BF16)
    return hi, (v - hi.astype(F32)).astype(BF16)


def nt(a, b):
    return lax.dot_general(a, b, (((1,), (1,)), ((), ())), preferred_element_type=F32)


def nt3(ah, al, bh, bl):
    return nt(ah, bh) + (nt(ah, bl) + nt(al, bh))


class Chan:
    def __init__(self, send, recv):
        self.send, self.recv = send, recv

    def copy(self, src, dst, idx, device):
        return pltpu.make_async_remote_copy(
            src_ref=src, dst_ref=dst, send_sem=self.send.at[idx], recv_sem=self.recv.at[idx],
            device_id=device, device_id_type=MESH,
        )


def front_kernel(
    mask_ref, slot_ref, far_ref, trail_ref, below_ref, pivot_ref, tiles_ref,
    schur_ref, panel_ref,
    apiv, own, mine, lhi, llo, xhi, xlo, rall, cur, bcur, inv_h, inv_l, tout, tin, iout, iin,
    p1s, p1r, p2s, p2r, p3s, p3r, p4s, p4r, o1s, o1r, o2s, o2r, m1s, m1r, m2s, m2r,
    ts, tr, rs, rr, qs, qr,
):
    sub = lax.axis_index("sub")
    grp = lax.axis_index("grp")
    y, zl, core = sub // 8, (sub // 2) % 4, sub % 2
    x, zh = grp // 2, grp % 2
    z = zh * 4 + zl
    mate = 1 - core
    me = zl * 2 + core

    def at(yy, zz, cc, xx, hh):
        return ((yy * 4 + zz) * 2 + cc, xx * 2 + hh)

    def z_dev(d):
        zz = (z + d) % 8
        return at(y, zz % 4, core, x, zz // 4)

    def y_dev(d):
        return at((y + d) % 8, zl, core, x, zh)

    def x_dev(d):
        return at(y, zl, core, (x + d) % 4, zh)

    def line_dev(d):
        return at(y, (zl + d) % 4, core, x, zh)

    mate_dev = at(y, zl, mate, x, zh)
    p1, p2, p3, p4 = Chan(p1s, p1r), Chan(p2s, p2r), Chan(p3s, p3r), Chan(p4s, p4r)
    o1, o2, m1, m2 = Chan(o1s, o1r), Chan(o2s, o2r), Chan(m1s, m1r), Chan(m2s, m2r)
    tc, rc, qc = Chan(ts, tr), Chan(rs, rr), Chan(qs, qr)

    keep = mask_ref[0].astype(F32)
    apiv[grp, y, core, pl.ds(zl * 16, 16), :] = pivot_ref[...]
    own[grp] = below_ref[...] * keep
    tout[...] = tiles_ref[...].astype(BF16)
    line = lax.broadcasted_iota(jnp.int32, (8, 128), 0)
    info = jnp.zeros((8, 128), F32)
    for u in range(2):
        info = jnp.where(line == u, slot_ref[u].astype(F32), info)
        info = jnp.where(line == 2 + u, far_ref[u].astype(F32), info)
    iout[...] = info

    barrier = pltpu.get_barrier_semaphore()

    def greet(device):
        pl.semaphore_signal(barrier, inc=1, device_id=device, device_id_type=MESH)

    for d in range(1, 8):
        greet(z_dev(d))
        greet(y_dev(d))
    for d in range(1, 4):
        greet(x_dev(d))
    greet(mate_dev)
    for g in range(8):
        @pl.when((grp != g) | (y != grp))
        def _():
            greet(at(grp, zl, core, g // 2, g % 2))
    pl.semaphore_wait(barrier, 26 - (y == grp).astype(jnp.int32))

    def p1_copy(d):
        ref = apiv.at[grp, y, core, pl.ds(zl * 16, 16)]
        return p1.copy(ref, ref, d - 1, z_dev(d))

    for d in range(1, 8):
        p1_copy(d).start()

    def o1_copy():
        return o1.copy(own.at[grp], own.at[grp], 0, at(y, zl, core, x, 1 - zh))

    def m1_copy(k):
        return m1.copy(
            own.at[grp, pl.ds(32 * k, 32)], mine.at[grp, k], grp, at(k, zl, core, y // 2, y % 2)
        )

    def m1_home(k):
        return pltpu.make_async_copy(own.at[grp, pl.ds(32 * k, 32)], mine.at[grp, k], m1r.at[grp])

    def m1_self(k):
        return (y == grp) & (y == k)

    o1_copy().start()
    for k in range(8):
        @pl.when(m1_self(k))
        def _():
            m1_home(k).start()

        @pl.when(jnp.logical_not(m1_self(k)))
        def _():
            m1_copy(k).start()

    def needed(g, yy):
        return (g < 4) | (yy >= 4)

    def p2_copy(d, h, yy):
        ref = apiv.at[2 * x + h, yy, core]
        return p2.copy(ref, ref, (d - 1, h), y_dev(d))

    for d in range(1, 8):
        zz = (z + 8 - d) % 8
        ref = apiv.at[2 * x + zz // 4, y, core, pl.ds((zz % 4) * 16, 16)]
        p1.copy(ref, ref, d - 1, z_dev(d)).wait_recv()
    for h in range(2):
        for d in range(1, 8):
            @pl.when(needed(2 * x + h, y))
            def _():
                p2_copy(d, h, y).start()

    def p3_copy(d, h, v, xx):
        ref = apiv.at[2 * xx + h, pl.ds(4 * v, 4), core]
        return p3.copy(ref, ref, (d - 1, h, v), x_dev(d))

    for h in range(2):
        for v in range(2):
            @pl.when(needed(2 * x + h, 4 * v))
            def _():
                for yy in range(4 * v, 4 * v + 4):
                    @pl.when(y != yy)
                    def _():
                        d = (y + 8 - yy) % 8
                        p2_copy(d, h, yy).wait_recv()
                for d in range(1, 4):
                    p3_copy(d, h, v, x).start()

    def m2_copy(d, h, yy):
        ref = mine.at[pl.ds(4 * h, 4), yy]
        return m2.copy(ref, ref, (d - 1, h), y_dev(d))

    def o2_copy(d, xx):
        ref = own.at[pl.ds(2 * xx, 2)]
        return o2.copy(ref, ref, d - 1, x_dev(d))

    def t_copies():
        far_dev = y_dev(4)
        return (tc.copy(tout, tin, 0, far_dev), tc.copy(iout, iin, 1, far_dev))

    def start_rows():
        o1.copy(own.at[grp], own.at[x * 2 + 1 - zh], 0, at(y, zl, core, x, 1 - zh)).wait_recv()
        for d in range(1, 4):
            o2_copy(d, x).start()
        for g in range(8):
            m1.copy(own.at[0, pl.ds(0, 32)], mine.at[g, y], g, mate_dev).wait_recv()
        for h in range(2):
            for d in range(1, 8):
                m2_copy(d, h, y).start()

    def p4_copy(g, half):
        ref = apiv.at[g, :, half]
        return p4.copy(ref, ref, g, mate_dev)

    def forward(g):
        d = (x + 4 - g // 2) % 4

        @pl.when(d != 0)
        def _():
            for v in range(2):
                @pl.when(needed(g, 4 * v))
                def _():
                    p3_copy(d, g % 2, v, g // 2).wait_recv()

        p4_copy(g, core).start()

    def arrived(g):
        p4_copy(g, mate).wait_recv()

    def column(g):
        return apiv[g].reshape(8, 2, 4, 16, 128).swapaxes(1, 2).reshape(1024, 128)

    def r_copy(d, j, who):
        ref = rall.at[j, who]
        return rc.copy(ref, ref, (d - 1, j), line_dev(d))

    def q_copy(i, j, who):
        ref = rall.at[j, who]
        return qc.copy(ref, ref, (i, j), mate_dev)

    def line_row(d, cc):
        return ((zl + 4 - d) % 4) * 2 + cc

    def send_rows(j):
        for d in range(1, 4):
            r_copy(d, j, me).start()
        q_copy(0, j, me).start()

    def pass_rows(j):
        for d in range(1, 4):
            r_copy(d, j, line_row(d, core)).wait_recv()
            q_copy(d, j, line_row(d, core)).start()

    def rows_arrived(j):
        for d in range(4):
            q_copy(d, j, line_row(d, mate)).wait_recv()

    def solve_rows(j):
        at_j = pl.ds(pl.multiple_of(j * 128, 128), 128)
        rest = bcur[...] - nt3(xhi[...], xlo[...], lhi[at_j, :], llo[at_j, :])
        rh, rl = split(rest)
        return nt3(rh, rl, inv_h[...], inv_l[...])

    def keep_rows(j, sol):
        at_j = pl.ds(pl.multiple_of(j * 128, 128), 128)
        sh, sl = split(sol)
        xhi[:, at_j] = sh
        xlo[:, at_j] = sl
        rall[j, me] = sh[256:]

        @pl.when(grp == j)
        def _():
            panel_ref[...] = sol[:256]

        send_rows(j)

    def take_rows(j):
        @pl.when(j % 2 == 0)
        def _():
            d = (x + 4 - j // 2) % 4

            @pl.when(d != 0)
            def _():
                o2_copy(d, j // 2).wait_recv()

        for h in range(2):
            @pl.when(j == 4 * h)
            def _():
                for d in range(1, 8):
                    m2_copy(d, h, (y + 8 - d) % 8).wait_recv()

        bcur[:256, :] = own[j]
        bcur[256:, :] = mine[j].reshape(256, 128)

    zero = jnp.zeros((1024, 1024), BF16)
    lhi[...] = zero
    llo[...] = zero
    xhi[...] = jnp.zeros((512, 1024), BF16)
    xlo[...] = jnp.zeros((512, 1024), BF16)
    bcur[...] = jnp.zeros((512, 128), F32)
    inv_h[...] = jnp.zeros((128, 128), BF16)
    inv_l[...] = jnp.zeros((128, 128), BF16)
    rows = lax.broadcasted_iota(jnp.int32, (1024, 128), 0)

    forward(0)
    start_rows()
    forward(1)
    arrived(0)
    cur[...] = column(0)

    def step(j, _):
        nxt = jnp.minimum(j + 1, 7)
        at_j = pl.ds(pl.multiple_of(j * 128, 128), 128)
        at_n = pl.ds(pl.multiple_of(nxt * 128, 128), 128)
        inv = inverse_factor(cur[at_j, :])
        past = nt3(lhi[...], llo[...], lhi[at_n, :], llo[at_n, :])
        sol = solve_rows(jnp.maximum(j - 1, 0))

        @pl.when(j >= 1)
        def _():
            keep_rows(j - 1, sol)

        @pl.when(j == 2)
        def _():
            for copy in t_copies():
                copy.start()

        @pl.when(j >= 2)
        def _():
            pass_rows(j - 2)

        @pl.when(j < 6)
        def _():
            forward(j + 2)

        take_rows(j)

        @pl.when(j < 7)
        def _():
            arrived(j + 1)

        ih, il = split(inv)
        inv_h[...] = ih
        inv_l[...] = il

        @pl.when(j < 7)
        def _():
            ch, cl = split(cur[...])
            low = jnp.where(rows >= (j + 1) * 128, nt3(ch, cl, ih, il), 0.0)
            lh, ll = split(low)
            lhi[:, at_j] = lh
            llo[:, at_j] = ll
            cur[...] = (column(nxt) - past) - nt3(lh, ll, lhi[at_n, at_j], llo[at_n, at_j])

        return 0

    lax.fori_loop(0, 8, step, 0)
    keep_rows(7, solve_rows(7))
    pass_rows(6)

    for copy in t_copies():
        copy.wait_recv()
    for j in range(7):
        rows_arrived(j)

    def weight(slots, flags, u, q, want):
        s, f = slots[u : u + 1, 0:1], flags[u : u + 1, 0:1]
        return jnp.where((s == q) & (f == want), 1.0, 0.0)

    def product(q, j0, j1):
        other = [rall[j, q] for j in range(j0, j1)]
        other = other[0] if len(other) == 1 else jnp.concatenate(other, axis=1)
        return nt(xhi[:256, 128 * j0 : 128 * j1], other)

    def first(q, _):
        qf = q.astype(F32)
        cols = pl.ds(pl.multiple_of(q * 256, 256), 256)
        near_s, near_f = iout[0:2, :], iout[2:4, :]
        far_s, far_f = iin[0:2, :], iin[2:4, :]
        acc = trail_ref[:, cols] - product(q, 0, 7)
        for u in range(2):
            acc = acc + weight(near_s, near_f, u, qf, 0.0) * tiles_ref[u]
            acc = acc + weight(far_s, far_f, u, qf, 1.0) * tin[u].astype(F32)
        schur_ref[:, cols] = acc
        return 0

    lax.fori_loop(0, 8, first, 0)
    pass_rows(7)
    rows_arrived(7)

    def second(q, _):
        cols = pl.ds(pl.multiple_of(q * 256, 256), 256)
        schur_ref[:, cols] = schur_ref[:, cols] - product(q, 7, 8)
        return 0

    lax.fori_loop(0, 8, second, 0)

    for d in range(1, 8):
        p1_copy(d).wait_send()
        for h in range(2):
            m2_copy(d, h, y).wait_send()

            @pl.when(needed(2 * x + h, y))
            def _():
                p2_copy(d, h, y).wait_send()
    for d in range(1, 4):
        o2_copy(d, x).wait_send()
        for h in range(2):
            for v in range(2):
                @pl.when(needed(2 * x + h, 4 * v))
                def _():
                    p3_copy(d, h, v, x).wait_send()
    o1_copy().wait_send()
    for k in range(8):
        @pl.when(jnp.logical_not(m1_self(k)))
        def _():
            m1_copy(k).wait_send()
    for copy in t_copies():
        copy.wait_send()

    def sent(j, _):
        p4_copy(j, core).wait_send()
        for d in range(1, 4):
            r_copy(d, j, me).wait_send()
            q_copy(d, j, line_row(d, core)).wait_send()
        q_copy(0, j, me).wait_send()
        return 0

    lax.fori_loop(0, 8, sent, 0)


def body(front_trail, front_below, front_pivot, panel_mask, child_tiles, child_slot, child_far):
    smem = pl.BlockSpec(memory_space=pltpu.SMEM)
    vmem = pl.BlockSpec(memory_space=pltpu.VMEM)
    dma = pltpu.SemaphoreType.DMA
    pairs = [(7,), (7, 2), (3, 2, 2), (8,), (1,), (3,), (8,), (7, 2), (2,), (3, 8), (4, 8)]
    return pl.pallas_call(
        front_kernel,
        in_specs=[smem] * 3 + [vmem] * 4,
        out_specs=[vmem, vmem],
        out_shape=[
            jax.ShapeDtypeStruct(front_trail.shape, F32),
            jax.ShapeDtypeStruct(front_below.shape, F32),
        ],
        scratch_shapes=[
            pltpu.VMEM((8, 8, 2, 64, 128), F32),
            pltpu.VMEM((8, 256, 128), F32),
            pltpu.VMEM((8, 8, 32, 128), F32),
            pltpu.VMEM((1024, 1024), BF16),
            pltpu.VMEM((1024, 1024), BF16),
            pltpu.VMEM((512, 1024), BF16),
            pltpu.VMEM((512, 1024), BF16),
            pltpu.VMEM((8, 8, 256, 128), BF16),
            pltpu.VMEM((1024, 128), F32),
            pltpu.VMEM((512, 128), F32),
            pltpu.VMEM((128, 128), BF16),
            pltpu.VMEM((128, 128), BF16),
            pltpu.VMEM((2, 256, 256), BF16),
            pltpu.VMEM((2, 256, 256), BF16),
            pltpu.VMEM((8, 128), F32),
            pltpu.VMEM((8, 128), F32),
        ]
        + [dma(shape) for shape in pairs for _ in range(2)],
        compiler_params=pltpu.CompilerParams(
            collective_id=0, has_side_effects=True, vmem_limit_bytes=60 * 2**20
        ),
        cost_estimate=pl.CostEstimate(
            flops=6_000_000_000, bytes_accessed=6_000_000, transcendentals=0
        ),
        name="front",
    )(
        panel_mask,
        child_slot.reshape(2),
        child_far.reshape(2),
        front_trail,
        front_below,
        front_pivot,
        child_tiles.reshape(2, 256, 256),
    )


def solution(mesh):
    return jax.shard_map(
        body,
        mesh=mesh,
        in_specs=(
            P("sub", "grp"),
            P("sub", "grp"),
            P("sub", "grp"),
            P("sub"),
            P("sub", "grp", None, None, None),
            P("sub", "grp", None),
            P("sub", "grp", None),
        ),
        out_specs=(P("sub", "grp"), P("sub", "grp")),
        check_vma=False,
    )
```

```python
import jax
import jax.numpy as jnp
from jax import lax
from jax.experimental import pallas as pl
from jax.experimental.pallas import tpu as pltpu
from jax.sharding import PartitionSpec as P

F32, BF16 = jnp.float32, jnp.bfloat16
MESH = pl.DeviceIdType.MESH
NB = 8


def row_of(v, r):
    return jnp.broadcast_to(v[r : r + 1, :], v.shape)


def lane_of(v, c):
    return jnp.broadcast_to(v[:, c : c + 1], v.shape)


def inverse_factor(block):
    strips = block.shape[0] // 8
    width = block.shape[1]
    sub = lax.broadcasted_iota(jnp.int32, (8, width), 0)
    lane = lax.broadcasted_iota(jnp.int32, (8, width), 1)
    unit = [(lane == sub + 8 * t).astype(F32) for t in range(strips)]
    left = [block[8 * t : 8 * t + 8, :] for t in range(strips)]
    out = []
    for k in range(strips):
        pivot, jordan, forward = left[k], unit[k], unit[k]
        cols = [lane_of(pivot, 8 * k + c) for c in range(8)]
        diag = jnp.ones((8, width), F32)
        for r in range(0, 8, 2):
            a = row_of(cols[r], r)
            b = row_of(cols[r], r + 1)
            d = row_of(cols[r + 1], r + 1)
            det = a * d - b * b
            over = 1.0 / det
            over_a = 1.0 / a
            ia, ib, id_ = d * over, -b * over, a * over
            is0, is1 = sub == r, sub == r + 1
            pair = is0 | is1
            g0 = jnp.where(is0, -ia, jnp.where(is1, -ib, cols[r] * ia + cols[r + 1] * ib))
            g1 = jnp.where(is0, -ib, jnp.where(is1, -id_, cols[r] * ib + cols[r + 1] * id_))
            f0, f1 = row_of(forward, r), row_of(forward, r + 1)
            forward = jnp.where(
                sub > r + 1,
                forward - g0 * f0 - g1 * f1,
                jnp.where(is1, forward - (b * over_a) * f0, forward),
            )
            diag = jnp.where(is0, a, jnp.where(is1, det * over_a, diag))

            def step(v):
                return (jnp.where(pair, 0.0, v) - g0 * row_of(v, r)) - g1 * row_of(v, r + 1)

            for c in range(r + 2, 8):
                cols[c] = step(cols[c])
            jordan, pivot = step(jordan), step(pivot)
        out.append(forward * lax.rsqrt(diag))
        prow = [row_of(pivot, c) for c in range(8)]
        jrow = [row_of(jordan, c) for c in range(8)]
        for t in range(k + 1, strips):
            coef = [lane_of(left[t], 8 * k + c) for c in range(8)]

            def total(q):
                p = [coef[c] * q[c] for c in range(8)]
                return ((p[0] + p[1]) + (p[2] + p[3])) + ((p[4] + p[5]) + (p[6] + p[7]))

            left[t] = left[t] - total(prow)
            unit[t] = unit[t] - total(jrow)
    return jnp.concatenate(out, axis=0)


def split(v):
    hi = v.astype(BF16)
    return hi, (v - hi.astype(F32)).astype(BF16)


def nt(a, b):
    return lax.dot_general(a, b, (((1,), (1,)), ((), ())), preferred_element_type=F32)


def nt3(ah, al, bh, bl):
    return nt(ah, bh) + (nt(ah, bl) + nt(al, bh))


class Chan:
    def __init__(self, send, recv):
        self.send, self.recv = send, recv

    def copy(self, src, dst, idx, device):
        return pltpu.make_async_remote_copy(
            src_ref=src, dst_ref=dst, send_sem=self.send.at[idx], recv_sem=self.recv.at[idx],
            device_id=device, device_id_type=MESH,
        )


def front_kernel(
    mask_ref, slot_ref, far_ref, below_ref, pivot_ref, tiles_ref,
    delta_ref, panel_ref,
    apiv, kept, own, mine, lhi, llo, xhi, xlo, rall, cur, diag, bcur, inv_h, inv_l, tout, tin, iout, iin, acc,
    p1s, p1r, p2s, p2r, p3s, p3r, p4s, p4r, o1s, o1r, o2s, o2r, m1s, m1r, m2s, m2r,
    ts, tr, rs, rr, us, ur, qs, qr, out_sem, home_sem,
):
    sub = lax.axis_index("sub")
    grp = lax.axis_index("grp")
    y, zl, core = sub // 8, (sub // 2) % 4, sub % 2
    x, zh = grp // 2, grp % 2
    z = zh * 4 + zl
    mate = 1 - core

    def at(yy, zz, cc, xx, hh):
        return ((yy * 4 + zz) * 2 + cc, xx * 2 + hh)

    def y_dev(d):
        return at((y + d) % 8, zl, core, x, zh)

    def x_dev(d):
        return at(y, zl, core, (x + d) % 4, zh)

    def grp_dev(d):
        g = (grp + d) % 8
        return at(y, zl, core, g // 2, g % 2)

    def line_dev(d):
        return at(y, (zl + d) % 4, core, x, zh)

    mate_dev = at(y, zl, mate, x, zh)
    p1, p2, p3, p4 = Chan(p1s, p1r), Chan(p2s, p2r), Chan(p3s, p3r), Chan(p4s, p4r)
    o1, o2, m1, m2 = Chan(o1s, o1r), Chan(o2s, o2r), Chan(m1s, m1r), Chan(m2s, m2r)
    tc, rc, uc, qc = Chan(ts, tr), Chan(rs, rr), Chan(us, ur), Chan(qs, qr)

    barrier = pltpu.get_barrier_semaphore()

    def greet(device):
        pl.semaphore_signal(barrier, inc=1, device_id=device, device_id_type=MESH)

    for d in range(1, 8):
        greet(y_dev(d))
    for d in range(1, 4):
        greet(line_dev(d))
    for d in range(1, 8):
        greet(grp_dev(d))
    for g in range(8):
        @pl.when((g != grp) | (x != zl))
        def _():
            greet(at(y, x, core, g // 2, g % 2))
    greet(mate_dev)
    for g in range(8):
        @pl.when((grp != g) | (y != grp))
        def _():
            greet(at(grp, zl, core, g // 2, g % 2))

    keep = mask_ref[0].astype(F32)
    kept[...] = below_ref[...] * keep
    tout[...] = tiles_ref[...].astype(BF16)
    line = lax.broadcasted_iota(jnp.int32, (8, 128), 0)
    info = jnp.zeros((8, 128), F32)
    for u in range(2):
        info = jnp.where(line == u, slot_ref[u].astype(F32), info)
        info = jnp.where(line == 2 + u, far_ref[u].astype(F32), info)
    iout[...] = info

    zero = jnp.zeros((1024, 1024), BF16)
    lhi[...] = zero
    llo[...] = zero
    xhi[...] = jnp.zeros((384, 1024), BF16)
    xlo[...] = jnp.zeros((384, 1024), BF16)
    cur[...] = jnp.zeros((1024, 128), F32)
    bcur[...] = jnp.zeros((384, 128), F32)
    inv_h[...] = jnp.zeros((8, 128, 128), BF16)
    inv_l[...] = jnp.zeros((8, 128, 128), BF16)
    pl.semaphore_wait(
        barrier, 34 - (y == grp).astype(jnp.int32) - (x == zl).astype(jnp.int32)
    )

    def p1_copy(zz):
        return p1.copy(
            pivot_ref, apiv.at[grp, y, core, zl], grp, at(y, zz % 4, core, zl, zz // 4)
        )

    def p1_self(zz):
        return (x == zl) & (z == zz)

    def p1_home():
        return pltpu.make_async_copy(pivot_ref, apiv.at[grp, y, core, zl], p1r.at[grp])

    for zz in range(8):
        @pl.when(jnp.logical_not(p1_self(zz)))
        def _():
            p1_copy(zz).start()

    @pl.when(x == zl)
    def _():
        p1_home().start()

    spans = ((0, 1, 0), (1, 1, 1), (2, 2, 2), (4, 4, 4))

    def p2_copy(d, i, yy):
        ref = apiv.at[pl.ds(*spans[i][:2]), yy, core, x]
        return p2.copy(ref, ref, (d - 1, i), y_dev(d))

    for g in range(8):
        p1.copy(pivot_ref, apiv.at[g, y, core, x], g, mate_dev).wait_recv()
    for i in range(4):
        @pl.when(y >= spans[i][2])
        def _():
            for d in range(1, 8):
                p2_copy(d, i, y).start()

    def o1_copy(d):
        quarter = ((grp + d) % 8) // 2
        return o1.copy(
            kept.at[pl.ds(64 * quarter, 64)], own.at[grp, quarter], d - 1, grp_dev(d)
        )

    def o1_home():
        return pltpu.make_async_copy(kept.at[pl.ds(64 * x, 64)], own.at[grp, x], home_sem)

    def m1_copy(k):
        return m1.copy(
            kept.at[pl.ds(32 * k, 32)], mine.at[grp, k // 2], grp, at(k, zl, core, y // 2, y % 2)
        )

    def m1_home(k):
        return pltpu.make_async_copy(
            kept.at[pl.ds(32 * k, 32)], mine.at[grp, k // 2], m1r.at[grp]
        )

    def m1_self(k):
        return (y == grp) & (y == k)

    for d in range(1, 8):
        o1_copy(d).start()
    o1_home().start()
    for k in range(8):
        @pl.when(m1_self(k))
        def _():
            m1_home(k).start()

        @pl.when(jnp.logical_not(m1_self(k)))
        def _():
            m1_copy(k).start()

    items = ((0, 0, 1), (0, 1, 7), (1, 1, 7), (2, 2, 6), (3, 4, 4))

    def p3_copy(d, i, xx):
        span, first, count = items[i]
        ref = apiv.at[pl.ds(*spans[span][:2]), pl.ds(first, count), core, xx]
        return p3.copy(ref, ref, (d - 1, i), x_dev(d))

    def spread(i):
        span, first, count = items[i]
        for yy in range(first, first + count):
            @pl.when(y != yy)
            def _():
                p2_copy((y + 8 - yy) % 8, span, yy).wait_recv()
        for d in range(1, 4):
            p3_copy(d, i, x).start()

    groups = ((0, 2), (2, 3), (5, 3))

    def m2_copy(d, h, yy):
        ref = mine.at[pl.ds(*groups[h]), yy // 2]
        return m2.copy(ref, ref, (d - 1, h), y_dev(2 * d))

    def o2_copy(d, h, xx):
        ref = own.at[pl.ds(*groups[h]), xx]
        return o2.copy(ref, ref, (d - 1, h), x_dev(d))

    def t_copies():
        far_dev = y_dev(4)
        return (tc.copy(tout, tin, 0, far_dev), tc.copy(iout, iin, 1, far_dev))

    def rows_here():
        o1_home().wait()
        for d in range(1, 8):
            o1.copy(
                kept.at[pl.ds(0, 64)], own.at[(grp + 8 - d) % 8, x], d - 1, grp_dev(d)
            ).wait_recv()
        for g in range(8):
            m1.copy(kept.at[pl.ds(0, 32)], mine.at[g, y // 2], g, mate_dev).wait_recv()

    def start_rows(h):
        for d in range(1, 4):
            m2_copy(d, h, y).start()
            o2_copy(d, h, x).start()

    def p4_copy(i, half):
        span, first, count = items[i]
        ref = apiv.at[pl.ds(*spans[span][:2]), pl.ds(first, count), half]
        return p4.copy(ref, ref, i, mate_dev)

    def forward(i):
        for d in range(1, 4):
            p3_copy(d, i, (x + 4 - d) % 4).wait_recv()
        p4_copy(i, core).start()

    def arrived(i):
        p4_copy(i, mate).wait_recv()

    def natural(v):
        n = v.shape[0]
        return v.swapaxes(1, 2).reshape(n * 128, 128)

    def column(g):
        return natural(apiv[g])

    def diagonal(g):
        return natural(apiv[g, pl.ds(g, 1)])

    side = y % 2

    def r_copy(d, j, row):
        ref = rall.at[j, core, side, row]
        return rc.copy(ref, ref, (d - 1, j), line_dev(d))

    def u_copy(i, j, par):
        ref = rall.at[j, core, par, pl.ds(2 * i, 2)]
        return uc.copy(ref, ref, (i, j), y_dev((1, 7)[i]))

    def q_copy(i, j, par, half):
        ref = rall.at[j, half, par]
        return qc.copy(ref, ref, (i, j), mate_dev)

    def send_rows(j):
        for d in range(1, 4):
            r_copy(d, j, zl).start()

    def pass_rows(j):
        for d in range(1, 4):
            r_copy(d, j, (zl + 4 - d) % 4).wait_recv()
        for i in range(2):
            u_copy(i, j, side).start()
        q_copy(0, j, side, core).start()

    def pass_more(j):
        for i in range(2):
            u_copy(i, j, 1 - side).wait_recv()
        q_copy(1, j, 1 - side, core).start()

    def rows_arrived(j):
        q_copy(0, j, side, mate).wait_recv()
        q_copy(1, j, 1 - side, mate).wait_recv()

    def solve_rows(j):
        at_j = pl.ds(pl.multiple_of(j * 128, 128), 128)
        rest = bcur[...] - nt3(xhi[...], xlo[...], lhi[at_j, :], llo[at_j, :])
        rh, rl = split(rest)
        return nt3(rh, rl, inv_h[j], inv_l[j])

    def keep_rows(j, sol):
        at_j = pl.ds(pl.multiple_of(j * 128, 128), 128)
        sh, sl = split(sol)
        xhi[:, at_j] = sh
        xlo[:, at_j] = sl
        rall[j, core, side, zl] = sh[256:].reshape(4, 32, 128)

        @pl.when(grp == j)
        def _():
            panel_ref[...] = sol[:256]

        send_rows(j)

    def take_rows(j):
        for h in range(3):
            @pl.when(j == groups[h][0])
            def _():
                for d in range(1, 4):
                    m2_copy(d, h, (y + 8 - 2 * d) % 8).wait_recv()
                    o2_copy(d, h, (x + 4 - d) % 4).wait_recv()

        bcur[:256, :] = own[j].reshape(256, 128)
        bcur[256:, :] = mine[j].reshape(128, 128)

    rows = lax.broadcasted_iota(jnp.int32, (1024, 128), 0)

    for i in range(3):
        spread(i)
    forward(0)
    spread(3)
    arrived(0)
    diag[...] = diagonal(0)

    def step(j, _):
        last = jnp.maximum(j - 1, 0)
        nxt = jnp.minimum(j + 1, 7)
        at_l = pl.ds(pl.multiple_of(last * 128, 128), 128)
        at_j = pl.ds(pl.multiple_of(j * 128, 128), 128)
        at_n = pl.ds(pl.multiple_of(nxt * 128, 128), 128)
        inv = inverse_factor(diag[...])
        ch, cl = split(cur[...])
        low = jnp.where(rows >= j * 128, nt3(ch, cl, inv_h[last], inv_l[last]), 0.0)
        lh, ll = split(low)
        lhi[:, at_l] = lh
        llo[:, at_l] = ll
        past = nt3(lhi[...], llo[...], lhi[at_j, :], llo[at_j, :])
        past_n = nt3(lhi[at_n, :], llo[at_n, :], lhi[at_n, :], llo[at_n, :])
        done = jnp.where(j > 4, j - 1, jnp.maximum(j - 2, 0))
        sol = solve_rows(done)

        @pl.when(j >= 2)
        def _():
            keep_rows(done, sol)

        @pl.when(j == 0)
        def _():
            forward(1)
            forward(2)
            rows_here()
            start_rows(0)
            spread(4)
            arrived(1)
            arrived(2)

        @pl.when(j == 1)
        def _():
            forward(3)
            start_rows(1)
            start_rows(2)
            arrived(3)

        @pl.when(j == 2)
        def _():
            forward(4)

        @pl.when(j == 3)
        def _():
            arrived(4)

        ih, il = split(inv)
        inv_h[j] = ih
        inv_l[j] = il
        cur[...] = column(j) - past

        @pl.when(j < 7)
        def _():
            th, tl = split(cur[at_n, :])
            nh, nl = split(nt3(th, tl, ih, il))
            diag[...] = (diagonal(nxt) - past_n) - nt3(nh, nl, nh, nl)

        @pl.when(j == 3)
        def _():
            for copy in t_copies():
                copy.start()

        @pl.when((j >= 1) & (j < 5))
        def _():
            take_rows(j - 1)

        @pl.when(j == 4)
        def _():
            keep_rows(3, solve_rows(3))

        @pl.when(j >= 4)
        def _():
            take_rows(j)

        return 0

    def pass_at(j):
        @pl.when((j >= 3) & (j < 5))
        def _():
            pass_rows(j - 3)

        @pl.when(j == 4)
        def _():
            pass_more(0)

        @pl.when(j == 5)
        def _():
            pass_rows(2)
            pass_rows(3)
            pass_more(1)

        @pl.when(j == 6)
        def _():
            pass_rows(4)
            pass_more(2)
            pass_more(3)

        @pl.when(j == 7)
        def _():
            pass_rows(5)
            pass_more(4)

    def step_and_pass(j, _):
        step(j, 0)
        pass_at(j)
        return 0

    lax.fori_loop(0, 8, step_and_pass, 0)
    keep_rows(7, solve_rows(7))
    pass_rows(6)
    pass_more(5)

    for copy in t_copies():
        copy.wait_recv()
    for j in range(6):
        rows_arrived(j)

    def weight(slots, flags, u, q, want):
        s, f = slots[u : u + 1, 0:1], flags[u : u + 1, 0:1]
        return jnp.where((s == q) & (f == want), 1.0, 0.0)

    def product(q, j0, j1):
        zq, cq = q // 2, q % 2
        other = [rall[j, cq, :, zq].swapaxes(0, 1).reshape(256, 128) for j in range(j0, j1)]
        other = other[0] if len(other) == 1 else jnp.concatenate(other, axis=1)
        return nt(xhi[:256, 128 * j0 : 128 * j1], other)

    def first(q, _):
        qf = q.astype(F32)
        cols = pl.ds(pl.multiple_of(q * 256, 256), 256)
        near_s, near_f = iout[0:2, :], iout[2:4, :]
        far_s, far_f = iin[0:2, :], iin[2:4, :]
        total = -product(q, 0, 6)
        for u in range(2):
            total = total + weight(near_s, near_f, u, qf, 0.0) * tiles_ref[u]
            total = total + weight(far_s, far_f, u, qf, 1.0) * tin[u].astype(F32)
        acc[:, cols] = total
        return 0

    lax.fori_loop(0, 8, first, 0)
    pass_more(6)
    pass_rows(7)
    for zz in range(8):
        @pl.when(jnp.logical_not(p1_self(zz)))
        def _():
            p1_copy(zz).wait_send()
    for d in range(1, 4):
        for h in range(3):
            m2_copy(d, h, y).wait_send()
            o2_copy(d, h, x).wait_send()
    for i in range(4):
        @pl.when(y >= spans[i][2])
        def _():
            for d in range(1, 8):
                p2_copy(d, i, y).wait_send()
    for i in range(5):
        p4_copy(i, core).wait_send()
        for d in range(1, 4):
            p3_copy(d, i, x).wait_send()
    for d in range(1, 8):
        o1_copy(d).wait_send()
    for k in range(8):
        @pl.when(jnp.logical_not(m1_self(k)))
        def _():
            m1_copy(k).wait_send()
    for copy in t_copies():
        copy.wait_send()

    def sent(j, _):
        for d in range(1, 4):
            r_copy(d, j, zl).wait_send()
        for i in range(2):
            u_copy(i, j, side).wait_send()
        q_copy(0, j, side, core).wait_send()
        q_copy(1, j, 1 - side, core).wait_send()
        return 0

    lax.fori_loop(0, 7, sent, 0)
    pass_more(7)
    rows_arrived(6)
    rows_arrived(7)

    def out_copy(q):
        cols = pl.ds(pl.multiple_of(q * 256, 256), 256)
        return pltpu.make_async_copy(acc.at[:, cols], delta_ref.at[:, cols], out_sem.at[q])

    def second(q, _):
        cols = pl.ds(pl.multiple_of(q * 256, 256), 256)
        acc[:, cols] = acc[:, cols] - product(q, 6, 8)
        out_copy(q).start()
        return 0

    lax.fori_loop(0, 8, second, 0)
    sent(7, 0)
    for q in range(8):
        out_copy(q).wait()


def body(front_trail, front_below, front_pivot, panel_mask, child_tiles, child_slot, child_far):
    smem = pl.BlockSpec(memory_space=pltpu.SMEM)
    vmem = pl.BlockSpec(memory_space=pltpu.VMEM)
    dma = pltpu.SemaphoreType.DMA
    pairs = [(8,), (7, 4), (3, 5), (5,), (7,), (3, 3), (8,), (3, 3), (2,), (3, 8), (2, 8), (2, 8)]
    delta, panel = pl.pallas_call(
        front_kernel,
        in_specs=[smem] * 3 + [vmem] * 3,
        out_specs=[pl.BlockSpec(memory_space=pl.ANY), vmem],
        out_shape=[
            jax.ShapeDtypeStruct(front_trail.shape, F32),
            jax.ShapeDtypeStruct(front_below.shape, F32),
        ],
        scratch_shapes=[
            pltpu.VMEM((8, 8, 2, 4, 16, 128), F32),
            pltpu.VMEM((256, 128), F32),
            pltpu.VMEM((8, 4, 64, 128), F32),
            pltpu.VMEM((8, 4, 32, 128), F32),
            pltpu.VMEM((1024, 1024), BF16),
            pltpu.VMEM((1024, 1024), BF16),
            pltpu.VMEM((384, 1024), BF16),
            pltpu.VMEM((384, 1024), BF16),
            pltpu.VMEM((8, 2, 2, 4, 4, 32, 128), BF16),
            pltpu.VMEM((1024, 128), F32),
            pltpu.VMEM((128, 128), F32),
            pltpu.VMEM((384, 128), F32),
            pltpu.VMEM((8, 128, 128), BF16),
            pltpu.VMEM((8, 128, 128), BF16),
            pltpu.VMEM((2, 256, 256), BF16),
            pltpu.VMEM((2, 256, 256), BF16),
            pltpu.VMEM((8, 128), F32),
            pltpu.VMEM((8, 128), F32),
            pltpu.VMEM((256, 2048), F32),
        ]
        + [dma(shape) for shape in pairs for _ in range(2)]
        + [dma((8,)), dma],
        compiler_params=pltpu.CompilerParams(
            collective_id=0, has_side_effects=True, vmem_limit_bytes=60 * 2**20
        ),
        cost_estimate=pl.CostEstimate(
            flops=6_000_000_000, bytes_accessed=6_000_000, transcendentals=0
        ),
        name="front",
    )(
        panel_mask,
        child_slot.reshape(2),
        child_far.reshape(2),
        front_below,
        front_pivot,
        child_tiles.reshape(2, 256, 256),
    )
    return front_trail + delta, panel


def solution(mesh):
    return jax.shard_map(
        body,
        mesh=mesh,
        in_specs=(
            P("sub", "grp"),
            P("sub", "grp"),
            P("sub", "grp"),
            P("sub"),
            P("sub", "grp", None, None, None),
            P("sub", "grp", None),
            P("sub", "grp", None),
        ),
        out_specs=(P("sub", "grp"), P("sub", "grp")),
        check_vma=False,
    )
```

```python
import jax
import jax.numpy as jnp
from jax import lax
from jax.experimental import pallas as pl
from jax.experimental.pallas import tpu as pltpu
from jax.sharding import PartitionSpec as P

F32, BF16 = jnp.float32, jnp.bfloat16
MESH = pl.DeviceIdType.MESH
NB = 8


def row_of(v, r):
    return jnp.broadcast_to(v[r : r + 1, :], v.shape)


def lane_of(v, c):
    return jnp.broadcast_to(v[:, c : c + 1], v.shape)


def inverse_factor(block):
    strips = block.shape[0] // 8
    width = block.shape[1]
    sub = lax.broadcasted_iota(jnp.int32, (8, width), 0)
    lane = lax.broadcasted_iota(jnp.int32, (8, width), 1)
    unit = [(lane == sub + 8 * t).astype(F32) for t in range(strips)]
    left = [block[8 * t : 8 * t + 8, :] for t in range(strips)]
    out = []
    for k in range(strips):
        pivot, jordan, forward = left[k], unit[k], unit[k]
        cols = [lane_of(pivot, 8 * k + c) for c in range(8)]
        diag = jnp.ones((8, width), F32)
        for r in range(0, 8, 2):
            a = row_of(cols[r], r)
            b = row_of(cols[r], r + 1)
            d = row_of(cols[r + 1], r + 1)
            det = a * d - b * b
            over = 1.0 / det
            over_a = 1.0 / a
            ia, ib, id_ = d * over, -b * over, a * over
            is0, is1 = sub == r, sub == r + 1
            pair = is0 | is1
            g0 = jnp.where(is0, -ia, jnp.where(is1, -ib, cols[r] * ia + cols[r + 1] * ib))
            g1 = jnp.where(is0, -ib, jnp.where(is1, -id_, cols[r] * ib + cols[r + 1] * id_))
            f0, f1 = row_of(forward, r), row_of(forward, r + 1)
            forward = jnp.where(
                sub > r + 1,
                forward - g0 * f0 - g1 * f1,
                jnp.where(is1, forward - (b * over_a) * f0, forward),
            )
            diag = jnp.where(is0, a, jnp.where(is1, det * over_a, diag))

            def step(v):
                return (jnp.where(pair, 0.0, v) - g0 * row_of(v, r)) - g1 * row_of(v, r + 1)

            for c in range(r + 2, 8):
                cols[c] = step(cols[c])
            jordan, pivot = step(jordan), step(pivot)
        out.append(forward * lax.rsqrt(diag))
        prow = [row_of(pivot, c) for c in range(8)]
        jrow = [row_of(jordan, c) for c in range(8)]
        for t in range(k + 1, strips):
            coef = [lane_of(left[t], 8 * k + c) for c in range(8)]

            def total(q):
                p = [coef[c] * q[c] for c in range(8)]
                return ((p[0] + p[1]) + (p[2] + p[3])) + ((p[4] + p[5]) + (p[6] + p[7]))

            left[t] = left[t] - total(prow)
            unit[t] = unit[t] - total(jrow)
    return jnp.concatenate(out, axis=0)


def split(v):
    hi = v.astype(BF16)
    return hi, (v - hi.astype(F32)).astype(BF16)


def nt(a, b):
    return lax.dot_general(a, b, (((1,), (1,)), ((), ())), preferred_element_type=F32)


def nt3(ah, al, bh, bl):
    return nt(ah, bh) + (nt(ah, bl) + nt(al, bh))


class Chan:
    def __init__(self, send, recv):
        self.send, self.recv = send, recv

    def copy(self, src, dst, idx, device):
        return pltpu.make_async_remote_copy(
            src_ref=src, dst_ref=dst, send_sem=self.send.at[idx], recv_sem=self.recv.at[idx],
            device_id=device, device_id_type=MESH,
        )


def front_kernel(
    mask_ref, slot_ref, far_ref, below_ref, pivot_ref, tiles_ref,
    delta_ref, panel_ref,
    apiv, kept, own, mine, lhi, llo, xhi, xlo, rall, cur, diag, bcur, inv_h, inv_l, tout, tin, iout, iin, acc,
    p1s, p1r, p2s, p2r, p3s, p3r, p4s, p4r, o1s, o1r, o2s, o2r, m1s, m1r, m2s, m2r,
    ts, tr, rs, rr, us, ur, qs, qr, out_sem, home_sem,
):
    sub = lax.axis_index("sub")
    grp = lax.axis_index("grp")
    y, zl, core = sub // 8, (sub // 2) % 4, sub % 2
    x, zh = grp // 2, grp % 2
    z = zh * 4 + zl
    mate = 1 - core

    def at(yy, zz, cc, xx, hh):
        return ((yy * 4 + zz) * 2 + cc, xx * 2 + hh)

    def y_dev(d):
        return at((y + d) % 8, zl, core, x, zh)

    def x_dev(d):
        return at(y, zl, core, (x + d) % 4, zh)

    def grp_dev(d):
        g = (grp + d) % 8
        return at(y, zl, core, g // 2, g % 2)

    def line_dev(d):
        return at(y, (zl + d) % 4, core, x, zh)

    mate_dev = at(y, zl, mate, x, zh)
    p1, p2, p3, p4 = Chan(p1s, p1r), Chan(p2s, p2r), Chan(p3s, p3r), Chan(p4s, p4r)
    o1, o2, m1, m2 = Chan(o1s, o1r), Chan(o2s, o2r), Chan(m1s, m1r), Chan(m2s, m2r)
    tc, rc, uc, qc = Chan(ts, tr), Chan(rs, rr), Chan(us, ur), Chan(qs, qr)

    barrier = pltpu.get_barrier_semaphore()

    def greet(device):
        pl.semaphore_signal(barrier, inc=1, device_id=device, device_id_type=MESH)

    for d in range(1, 8):
        greet(y_dev(d))
    for d in range(1, 4):
        greet(line_dev(d))
    for d in range(1, 8):
        greet(grp_dev(d))
    for g in range(8):
        @pl.when((g != grp) | (x != zl))
        def _():
            greet(at(y, x, core, g // 2, g % 2))
    greet(mate_dev)
    for g in range(8):
        @pl.when((grp != g) | (y != grp))
        def _():
            greet(at(grp, zl, core, g // 2, g % 2))

    keep = mask_ref[0].astype(F32)
    kept[...] = below_ref[...] * keep
    tout[...] = tiles_ref[...].astype(BF16)
    line = lax.broadcasted_iota(jnp.int32, (8, 128), 0)
    info = jnp.zeros((8, 128), F32)
    for u in range(2):
        info = jnp.where(line == u, slot_ref[u].astype(F32), info)
        info = jnp.where(line == 2 + u, far_ref[u].astype(F32), info)
    iout[...] = info

    zero = jnp.zeros((1024, 1024), BF16)
    lhi[...] = zero
    llo[...] = zero
    xhi[...] = jnp.zeros((384, 1024), BF16)
    xlo[...] = jnp.zeros((384, 1024), BF16)
    cur[...] = jnp.zeros((1024, 128), F32)
    bcur[...] = jnp.zeros((384, 128), F32)
    inv_h[...] = jnp.zeros((8, 128, 128), BF16)
    inv_l[...] = jnp.zeros((8, 128, 128), BF16)
    pl.semaphore_wait(
        barrier, 34 - (y == grp).astype(jnp.int32) - (x == zl).astype(jnp.int32)
    )

    def p1_copy(zz):
        return p1.copy(
            pivot_ref, apiv.at[grp, y, core, zl], grp, at(y, zz % 4, core, zl, zz // 4)
        )

    def p1_self(zz):
        return (x == zl) & (z == zz)

    def p1_home():
        return pltpu.make_async_copy(pivot_ref, apiv.at[grp, y, core, zl], p1r.at[grp])

    for zz in range(8):
        @pl.when(jnp.logical_not(p1_self(zz)))
        def _():
            p1_copy(zz).start()

    @pl.when(x == zl)
    def _():
        p1_home().start()

    spans = ((0, 1, 0), (1, 1, 1), (2, 2, 2), (4, 4, 4))

    def p2_copy(d, i, yy):
        ref = apiv.at[pl.ds(*spans[i][:2]), yy, core, x]
        return p2.copy(ref, ref, (d - 1, i), y_dev(d))

    for g in range(8):
        p1.copy(pivot_ref, apiv.at[g, y, core, x], g, mate_dev).wait_recv()
    for i in range(4):
        @pl.when(y >= spans[i][2])
        def _():
            for d in range(1, 8):
                p2_copy(d, i, y).start()

    def o1_copy(d):
        quarter = ((grp + d) % 8) // 2
        return o1.copy(
            kept.at[pl.ds(64 * quarter, 64)], own.at[grp, quarter], d - 1, grp_dev(d)
        )

    def o1_home():
        return pltpu.make_async_copy(kept.at[pl.ds(64 * x, 64)], own.at[grp, x], home_sem)

    def m1_copy(k):
        return m1.copy(
            kept.at[pl.ds(32 * k, 32)], mine.at[grp, k // 2], grp, at(k, zl, core, y // 2, y % 2)
        )

    def m1_home(k):
        return pltpu.make_async_copy(
            kept.at[pl.ds(32 * k, 32)], mine.at[grp, k // 2], m1r.at[grp]
        )

    def m1_self(k):
        return (y == grp) & (y == k)

    for d in range(1, 8):
        o1_copy(d).start()
    o1_home().start()
    for k in range(8):
        @pl.when(m1_self(k))
        def _():
            m1_home(k).start()

        @pl.when(jnp.logical_not(m1_self(k)))
        def _():
            m1_copy(k).start()

    items = ((0, 0, 1), (0, 1, 7), (1, 1, 7), (2, 2, 6), (3, 4, 4))

    def p3_copy(d, i, xx):
        span, first, count = items[i]
        ref = apiv.at[pl.ds(*spans[span][:2]), pl.ds(first, count), core, xx]
        return p3.copy(ref, ref, (d - 1, i), x_dev(d))

    def spread(i):
        span, first, count = items[i]
        for yy in range(first, first + count):
            @pl.when(y != yy)
            def _():
                p2_copy((y + 8 - yy) % 8, span, yy).wait_recv()
        for d in range(1, 4):
            p3_copy(d, i, x).start()

    groups = ((0, 2), (2, 3), (5, 3))

    def m2_copy(d, h, yy):
        ref = mine.at[pl.ds(*groups[h]), yy // 2]
        return m2.copy(ref, ref, (d - 1, h), y_dev(2 * d))

    def o2_copy(d, h, xx):
        ref = own.at[pl.ds(*groups[h]), xx]
        return o2.copy(ref, ref, (d - 1, h), x_dev(d))

    def t_copy(i):
        src, dst = (iout, iin) if i == 2 else (tout.at[i], tin.at[i])
        return tc.copy(src, dst, i, y_dev(4))

    def rows_here():
        o1_home().wait()
        for d in range(1, 8):
            o1.copy(
                kept.at[pl.ds(0, 64)], own.at[(grp + 8 - d) % 8, x], d - 1, grp_dev(d)
            ).wait_recv()
        for g in range(8):
            m1.copy(kept.at[pl.ds(0, 32)], mine.at[g, y // 2], g, mate_dev).wait_recv()

    def start_rows(h):
        for d in range(1, 4):
            m2_copy(d, h, y).start()
            o2_copy(d, h, x).start()

    def p4_copy(i, half):
        span, first, count = items[i]
        ref = apiv.at[pl.ds(*spans[span][:2]), pl.ds(first, count), half]
        return p4.copy(ref, ref, i, mate_dev)

    def forward(i):
        for d in range(1, 4):
            p3_copy(d, i, (x + 4 - d) % 4).wait_recv()
        p4_copy(i, core).start()

    def arrived(i):
        p4_copy(i, mate).wait_recv()

    def natural(v):
        n = v.shape[0]
        return v.swapaxes(1, 2).reshape(n * 128, 128)

    def column(g):
        return natural(apiv[g])

    def diagonal(g):
        return natural(apiv[g, pl.ds(g, 1)])

    side = y % 2

    def r_copy(d, j, row):
        ref = rall.at[j, core, side, row]
        return rc.copy(ref, ref, (d - 1, j), line_dev(d))

    def u_copy(i, j, par):
        ref = rall.at[j, core, par, pl.ds(2 * i, 2)]
        return uc.copy(ref, ref, (i, j), y_dev((1, 7)[i]))

    def q_copy(i, j, par, half):
        ref = rall.at[j, half, par]
        return qc.copy(ref, ref, (i, j), mate_dev)

    def send_rows(j):
        for d in range(1, 4):
            r_copy(d, j, zl).start()

    def pass_rows(j):
        for d in range(1, 4):
            r_copy(d, j, (zl + 4 - d) % 4).wait_recv()
        for i in range(2):
            u_copy(i, j, side).start()
        q_copy(0, j, side, core).start()

    def pass_more(j):
        for i in range(2):
            u_copy(i, j, 1 - side).wait_recv()
        q_copy(1, j, 1 - side, core).start()

    def rows_arrived(j):
        q_copy(0, j, side, mate).wait_recv()
        q_copy(1, j, 1 - side, mate).wait_recv()

    def solve_rows(j):
        at_j = pl.ds(pl.multiple_of(j * 128, 128), 128)
        rest = bcur[...] - nt3(xhi[...], xlo[...], lhi[at_j, :], llo[at_j, :])
        rh, rl = split(rest)
        return nt3(rh, rl, inv_h[j], inv_l[j])

    def keep_rows(j, sol):
        at_j = pl.ds(pl.multiple_of(j * 128, 128), 128)
        sh, sl = split(sol)
        xhi[:, at_j] = sh
        xlo[:, at_j] = sl
        rall[j, core, side, zl] = sh[256:].reshape(4, 32, 128)

        @pl.when(grp == j)
        def _():
            panel_ref[...] = sol[:256]

        send_rows(j)

    def take_rows(j):
        for h in range(3):
            @pl.when(j == groups[h][0])
            def _():
                for d in range(1, 4):
                    m2_copy(d, h, (y + 8 - 2 * d) % 8).wait_recv()
                    o2_copy(d, h, (x + 4 - d) % 4).wait_recv()

        bcur[:256, :] = own[j].reshape(256, 128)
        bcur[256:, :] = mine[j].reshape(128, 128)

    rows = lax.broadcasted_iota(jnp.int32, (1024, 128), 0)

    for i in range(3):
        spread(i)
    forward(0)
    spread(3)
    arrived(0)
    diag[...] = diagonal(0)

    def step(j, _):
        last = jnp.maximum(j - 1, 0)
        nxt = jnp.minimum(j + 1, 7)
        at_l = pl.ds(pl.multiple_of(last * 128, 128), 128)
        at_j = pl.ds(pl.multiple_of(j * 128, 128), 128)
        at_n = pl.ds(pl.multiple_of(nxt * 128, 128), 128)
        inv = inverse_factor(diag[...])
        ch, cl = split(cur[...])
        low = jnp.where(rows >= j * 128, nt3(ch, cl, inv_h[last], inv_l[last]), 0.0)
        lh, ll = split(low)
        lhi[:, at_l] = lh
        llo[:, at_l] = ll
        past = nt3(lhi[...], llo[...], lhi[at_j, :], llo[at_j, :])
        past_n = nt3(lhi[at_n, :], llo[at_n, :], lhi[at_n, :], llo[at_n, :])
        done = jnp.where(j > 4, j - 1, jnp.maximum(j - 2, 0))
        sol = solve_rows(done)

        @pl.when(j >= 2)
        def _():
            keep_rows(done, sol)

        @pl.when(j == 0)
        def _():
            forward(1)
            forward(2)
            rows_here()
            start_rows(0)
            spread(4)
            arrived(1)
            arrived(2)

        @pl.when(j == 1)
        def _():
            forward(3)
            start_rows(1)
            start_rows(2)
            arrived(3)

        @pl.when(j == 2)
        def _():
            forward(4)

        @pl.when(j == 3)
        def _():
            arrived(4)

        ih, il = split(inv)
        inv_h[j] = ih
        inv_l[j] = il
        cur[...] = column(j) - past

        @pl.when(j < 7)
        def _():
            th, tl = split(cur[at_n, :])
            nh, nl = split(nt3(th, tl, ih, il))
            diag[...] = (diagonal(nxt) - past_n) - nt3(nh, nl, nh, nl)

        @pl.when(j == 2)
        def _():
            t_copy(0).start()

        @pl.when(j == 4)
        def _():
            t_copy(1).start()
            t_copy(2).start()

        @pl.when((j >= 1) & (j < 5))
        def _():
            take_rows(j - 1)

        @pl.when(j == 4)
        def _():
            keep_rows(3, solve_rows(3))

        @pl.when(j >= 4)
        def _():
            take_rows(j)

        return 0

    def pass_at(j):
        @pl.when((j >= 3) & (j < 5))
        def _():
            pass_rows(j - 3)

        @pl.when(j == 4)
        def _():
            pass_more(0)

        @pl.when(j == 5)
        def _():
            pass_rows(2)
            pass_rows(3)
            pass_more(1)

        @pl.when(j == 6)
        def _():
            pass_rows(4)
            pass_more(2)
            pass_more(3)

        @pl.when(j == 7)
        def _():
            pass_rows(5)
            pass_more(4)

    def step_and_pass(j, _):
        step(j, 0)
        pass_at(j)
        return 0

    lax.fori_loop(0, 8, step_and_pass, 0)
    keep_rows(7, solve_rows(7))
    pass_rows(6)
    pass_more(5)

    pass_more(6)
    pass_rows(7)

    for i in range(3):
        t_copy(i).wait_recv()
    for j in range(6):
        rows_arrived(j)

    def weight(slots, flags, u, q, want):
        s, f = slots[u : u + 1, 0:1], flags[u : u + 1, 0:1]
        return jnp.where((s == q) & (f == want), 1.0, 0.0)

    def product(q, j0, j1):
        zq, cq = q // 2, q % 2
        other = [rall[j, cq, :, zq].swapaxes(0, 1).reshape(256, 128) for j in range(j0, j1)]
        other = other[0] if len(other) == 1 else jnp.concatenate(other, axis=1)
        return nt(xhi[:256, 128 * j0 : 128 * j1], other)

    def first(q, _):
        qf = q.astype(F32)
        cols = pl.ds(pl.multiple_of(q * 256, 256), 256)
        near_s, near_f = iout[0:2, :], iout[2:4, :]
        far_s, far_f = iin[0:2, :], iin[2:4, :]
        total = -product(q, 0, 6)
        for u in range(2):
            total = total + weight(near_s, near_f, u, qf, 0.0) * tiles_ref[u]
            total = total + weight(far_s, far_f, u, qf, 1.0) * tin[u].astype(F32)
        acc[:, cols] = total
        return 0

    lax.fori_loop(0, 8, first, 0)
    for zz in range(8):
        @pl.when(jnp.logical_not(p1_self(zz)))
        def _():
            p1_copy(zz).wait_send()
    for d in range(1, 4):
        for h in range(3):
            m2_copy(d, h, y).wait_send()
            o2_copy(d, h, x).wait_send()
    for i in range(4):
        @pl.when(y >= spans[i][2])
        def _():
            for d in range(1, 8):
                p2_copy(d, i, y).wait_send()
    for i in range(5):
        p4_copy(i, core).wait_send()
        for d in range(1, 4):
            p3_copy(d, i, x).wait_send()
    for d in range(1, 8):
        o1_copy(d).wait_send()
    for k in range(8):
        @pl.when(jnp.logical_not(m1_self(k)))
        def _():
            m1_copy(k).wait_send()
    for i in range(3):
        t_copy(i).wait_send()

    def sent(j, _):
        for d in range(1, 4):
            r_copy(d, j, zl).wait_send()
        for i in range(2):
            u_copy(i, j, side).wait_send()
        q_copy(0, j, side, core).wait_send()
        q_copy(1, j, 1 - side, core).wait_send()
        return 0

    lax.fori_loop(0, 7, sent, 0)
    pass_more(7)
    rows_arrived(6)
    rows_arrived(7)

    def out_copy(q):
        cols = pl.ds(pl.multiple_of(q * 256, 256), 256)
        return pltpu.make_async_copy(acc.at[:, cols], delta_ref.at[:, cols], out_sem.at[q])

    def second(q, _):
        cols = pl.ds(pl.multiple_of(q * 256, 256), 256)
        acc[:, cols] = acc[:, cols] - product(q, 6, 8)
        out_copy(q).start()
        return 0

    lax.fori_loop(0, 8, second, 0)
    sent(7, 0)
    for q in range(8):
        out_copy(q).wait()


def body(front_trail, front_below, front_pivot, panel_mask, child_tiles, child_slot, child_far):
    smem = pl.BlockSpec(memory_space=pltpu.SMEM)
    vmem = pl.BlockSpec(memory_space=pltpu.VMEM)
    dma = pltpu.SemaphoreType.DMA
    pairs = [(8,), (7, 4), (3, 5), (5,), (7,), (3, 3), (8,), (3, 3), (3,), (3, 8), (2, 8), (2, 8)]
    delta, panel = pl.pallas_call(
        front_kernel,
        in_specs=[smem] * 3 + [vmem] * 3,
        out_specs=[pl.BlockSpec(memory_space=pl.ANY), vmem],
        out_shape=[
            jax.ShapeDtypeStruct(front_trail.shape, F32),
            jax.ShapeDtypeStruct(front_below.shape, F32),
        ],
        scratch_shapes=[
            pltpu.VMEM((8, 8, 2, 4, 16, 128), F32),
            pltpu.VMEM((256, 128), F32),
            pltpu.VMEM((8, 4, 64, 128), F32),
            pltpu.VMEM((8, 4, 32, 128), F32),
            pltpu.VMEM((1024, 1024), BF16),
            pltpu.VMEM((1024, 1024), BF16),
            pltpu.VMEM((384, 1024), BF16),
            pltpu.VMEM((384, 1024), BF16),
            pltpu.VMEM((8, 2, 2, 4, 4, 32, 128), BF16),
            pltpu.VMEM((1024, 128), F32),
            pltpu.VMEM((128, 128), F32),
            pltpu.VMEM((384, 128), F32),
            pltpu.VMEM((8, 128, 128), BF16),
            pltpu.VMEM((8, 128, 128), BF16),
            pltpu.VMEM((2, 256, 256), BF16),
            pltpu.VMEM((2, 256, 256), BF16),
            pltpu.VMEM((8, 128), F32),
            pltpu.VMEM((8, 128), F32),
            pltpu.VMEM((256, 2048), F32),
        ]
        + [dma(shape) for shape in pairs for _ in range(2)]
        + [dma((8,)), dma],
        compiler_params=pltpu.CompilerParams(
            collective_id=0, has_side_effects=True, vmem_limit_bytes=60 * 2**20
        ),
        cost_estimate=pl.CostEstimate(
            flops=6_000_000_000, bytes_accessed=6_000_000, transcendentals=0
        ),
        name="front",
    )(
        panel_mask,
        child_slot.reshape(2),
        child_far.reshape(2),
        front_below,
        front_pivot,
        child_tiles.reshape(2, 256, 256),
    )
    return front_trail + delta, panel


def solution(mesh):
    return jax.shard_map(
        body,
        mesh=mesh,
        in_specs=(
            P("sub", "grp"),
            P("sub", "grp"),
            P("sub", "grp"),
            P("sub"),
            P("sub", "grp", None, None, None),
            P("sub", "grp", None),
            P("sub", "grp", None),
        ),
        out_specs=(P("sub", "grp"), P("sub", "grp")),
        check_vma=False,
    )
```
